32 devices in a mesh: tier: 4 (over x, core), tile: 8 (over z, y).
Axes of the slice: x: 2, y: 2, z: 4, core: 2. Of those that a mesh axis runs over, the one named last changes fastest.
Arguments:
- starting_warmth_rise: float32 [32, 96, 1024], P('tile', 'tier'), may hold values from -3 to 8
- substance_per_cell: int32 [32, 96, 1024], P('tile', 'tier'), may hold values from 0 to 7
- material_transport_rates: float32 [2, 8], replicated, may hold values from 0.2 to 2
- patch_region_label: int32 [8, 8], P('tile'), may hold values from 0 to 15, as said below
- static_power_per_area: float32 [4, 16], replicated, may hold values from 0.5 to 4
- warming_power_factor: float32 [4, 16], replicated, may hold values from 0.2 to 0.8
- stacking_solve_operator: float32 [96, 96], replicated, may hold values from 0 to 1
Outputs:
- final_temperature: float32 [32, 96, 1024], P('tile', 'tier')
- block_power: float32 [4, 16], P('tier')
The draws below stay inside these ranges and needn't reach their ends.
Inputs may be any that keep to these rules, and one draw needn't show every extreme that they name: `patch_region_label`: every block number names at least one tile.
All inputs are finite; a program needn't handle non-finite values.
Results may differ from the reference program's by a relative error of at most 0.0001.
Values sent between devices are 32-bit elements; how exact they have to be, the bound alone decides.
A program may use at most 64 MiB of HBM per device.

```python
import math
import jax
import jax.numpy as jnp
from jax import lax

ROWS = 4
NY = 1024
LEVELS = 96
TILE_COLS = 128
NMAT = 8
STEPS = 2
TIERS = 4
LEV = 24
NX = 32
NBLK = 16


def draw_starting_warmth_rise(key, part):
    key_one, key_two = jax.random.split(jax.random.fold_in(key, 11))
    ramp_up = (1.0 + 2.0 * jnp.arange(NX, dtype=jnp.float32) / (NX - 1))[:, None, None]
    rough_part = jax.random.uniform(key_one, (NX, LEVELS, NY), jnp.float32, 0.5, 1.5)
    noise_part = 0.3 * jnp.clip(jax.random.normal(key_two, (NX, LEVELS, NY), jnp.float32), -6.0, 6.0)
    return ramp_up * rough_part + noise_part


def draw_patch_region_label(key, part):
    key_one, key_two = jax.random.split(jax.random.fold_in(key, 23))
    tile_total = NX // ROWS * (NY // TILE_COLS)
    positions = jnp.arange(tile_total, dtype=jnp.int32)
    extra_ids = jax.random.randint(key_one, (tile_total,), 0, NBLK, dtype=jnp.int32)
    tile_ids = jnp.where(positions < NBLK, positions, extra_ids)
    shuffle = jax.random.permutation(key_two, tile_total)
    return tile_ids[shuffle].reshape(NX // ROWS, NY // TILE_COLS)


def draw_stacking_solve_operator(key, part):
    levels_pos = jnp.arange(LEVELS, dtype=jnp.float32)
    distance = jnp.abs(levels_pos[:, None] - levels_pos[None, :])
    kernel = jnp.exp(-distance / (2.0 * LEV))
    rough_part = jax.random.uniform(jax.random.fold_in(key, 37), (LEVELS, LEVELS), jnp.float32, 0.5, 1.5)
    scale_off = 0.45 / (1.5 * (1.0 + 4.0 * LEV))
    return scale_off * kernel * rough_part + 0.5 * jnp.eye(LEVELS, dtype=jnp.float32)


def touch_ends(values, key, smallest, high):
    longest = values.shape.index(max(values.shape))
    spots = []
    for shift in (0, 1):
        where = [jax.random.randint(jax.random.fold_in(key, axis), (), 0, length) for axis, length in enumerate(values.shape)]
        where[longest] = (where[longest] + shift) % values.shape[longest]
        spots.append(tuple(where))
    return values.at[spots[0]].set(smallest).at[spots[1]].set(high)


def setup_inputs(seed: int = 0) -> dict:
    key_list = jax.random.split(jax.random.key(seed), 8)
    starting_warmth_rise = draw_starting_warmth_rise(jax.random.fold_in(key_list[7], 71), 0)
    substance_per_cell = touch_ends(jax.random.randint(key_list[1], (NX, LEVELS, NY), 0, NMAT), jax.random.fold_in(key_list[1], 1), 0, NMAT - 1).astype(jnp.int32)
    material_transport_rates = jnp.clip(jnp.exp(jax.random.uniform(key_list[2], (2, NMAT), jnp.float32, math.log(0.2), math.log(2.0))), 0.2, 2.0)
    patch_region_label = draw_patch_region_label(jax.random.fold_in(key_list[7], 71), 0)
    static_power_per_area = jnp.clip(jnp.exp(jax.random.uniform(key_list[4], (TIERS, NBLK), jnp.float32, math.log(0.5), math.log(4.0))), 0.5, 4.0)
    warming_power_factor = jnp.clip(jax.random.uniform(key_list[5], (TIERS, NBLK), jnp.float32, 0.2, 0.8), 0.2, 0.8)
    stacking_solve_operator = draw_stacking_solve_operator(jax.random.fold_in(key_list[7], 71), 0)
    return dict(starting_warmth_rise=starting_warmth_rise, substance_per_cell=substance_per_cell, material_transport_rates=material_transport_rates, patch_region_label=patch_region_label, static_power_per_area=static_power_per_area, warming_power_factor=warming_power_factor, stacking_solve_operator=stacking_solve_operator)


LATERAL_RATE = 0.12
SOURCE_GAIN = 0.02


def pair_mean(cond_a, cond_b):
    return 2.0 * cond_a * cond_b / (cond_a + cond_b)


def lateral(padded, conduct):
    centre = padded[1:-1, :, 1:-1]
    sideways_coupling_rate = conduct[0, 1:-1, :, 1:-1]
    stacking_coupling_rate = conduct[1, 1:-1, :, 1:-1]
    flow_sum = pair_mean(sideways_coupling_rate, conduct[0, 2:, :, 1:-1]) * (padded[2:, :, 1:-1] - centre)
    flow_sum = flow_sum + pair_mean(sideways_coupling_rate, conduct[0, :-2, :, 1:-1]) * (padded[:-2, :, 1:-1] - centre)
    flow_sum = flow_sum + pair_mean(stacking_coupling_rate, conduct[1, 1:-1, :, 2:]) * (padded[1:-1, :, 2:] - centre)
    flow_sum = flow_sum + pair_mean(stacking_coupling_rate, conduct[1, 1:-1, :, :-2]) * (padded[1:-1, :, :-2] - centre)
    return centre + LATERAL_RATE * flow_sum


def reference(starting_warmth_rise, substance_per_cell, material_transport_rates, patch_region_label, static_power_per_area, warming_power_factor, stacking_solve_operator):
    sideways_coupling_rate = jnp.zeros(starting_warmth_rise.shape, jnp.float32)
    stacking_coupling_rate = jnp.zeros(starting_warmth_rise.shape, jnp.float32)
    for material in range(NMAT):
        is_material = substance_per_cell == material
        sideways_coupling_rate = jnp.where(is_material, material_transport_rates[0, material], sideways_coupling_rate)
        stacking_coupling_rate = jnp.where(is_material, material_transport_rates[1, material], stacking_coupling_rate)
    cond_pad = jnp.pad(jnp.stack([sideways_coupling_rate, stacking_coupling_rate]), ((0, 0), (1, 1), (0, 0), (1, 1)))
    tile_ids = patch_region_label.reshape(-1).astype(jnp.int32)
    tile_rows = NX // ROWS
    tile_cols = NY // TILE_COLS
    counts = jax.ops.segment_sum(jnp.ones(tile_ids.shape, jnp.float32), tile_ids, num_segments=NBLK) * float(ROWS * TILE_COLS)
    present_warming_state = starting_warmth_rise
    block_power = jnp.zeros((TIERS, NBLK), jnp.float32)
    for step_index in range(STEPS):
        active = present_warming_state[:, ::LEV, :]
        tile_sums = active.reshape(tile_rows, ROWS, TIERS, tile_cols, TILE_COLS).sum(axis=(1, 4))
        per_tile = jnp.transpose(tile_sums, (1, 0, 2)).reshape(TIERS, -1)
        block_sum = jax.vmap(lambda values: jax.ops.segment_sum(values, tile_ids, num_segments=NBLK))(per_tile)
        block_power = static_power_per_area * jnp.exp(warming_power_factor * block_sum / counts)
        tile_power = block_power[:, tile_ids].reshape(TIERS, tile_rows, tile_cols)
        cell_power = jnp.repeat(jnp.repeat(tile_power, ROWS, axis=1), TILE_COLS, axis=2)
        moved_field = lateral(jnp.pad(present_warming_state, ((1, 1), (0, 0), (1, 1))), cond_pad)
        moved_field = moved_field.at[:, ::LEV, :].add(SOURCE_GAIN * jnp.transpose(cell_power, (1, 0, 2)))
        present_warming_state = jnp.einsum("lm,xmy->xly", stacking_solve_operator, moved_field, precision=lax.Precision.HIGHEST)
    return present_warming_state, block_power
```

```python
import functools

import jax
import jax.numpy as jnp
from jax import lax
from jax.experimental import pallas as pl
from jax.experimental.pallas import tpu as pltpu
from jax.sharding import PartitionSpec as P

TILE_COLS = 128
LATERAL_RATE = 0.12
SOURCE_GAIN = 0.02
MESH = pl.DeviceIdType.MESH


def face(a, b):
    return (2.0 * LATERAL_RATE) * a * b / (a + b)


def solve(op, x):
    return jnp.dot(op, x, precision=lax.Precision.HIGHEST, preferred_element_type=jnp.float32)


def kernel(
    ntier, ntile, nblk,
    t_in, m_in, rates, labels, stat, fac, a_in,
    out, pw_out,
    halo_t, halo_m, mv, e_mat, e_mv, col_m, col_me, col_mh, col, col_e, t1, halo_1, mv2, res,
    cx, cy, cl, p1, p2a, p2b,
    s_halo, r_halo, s_a2a, r_a2a, s_mat, r_mat, s_me, r_me, s_e, r_e, s_out, r_out,
    s_p1, r_p1, s_pa, r_pa, s_pb, r_pb,
):
    tier = lax.axis_index("tier")
    tile = lax.axis_index("tile")
    rows, lev, width = t_in.shape
    cols = width // ntier
    quarter = cols // TILE_COLS
    levels = lev * ntier
    nmat = rates.shape[1]
    order = [r for r in range(1, rows - 1)] + [0, rows - 1]

    def tier_at(k):
        return lax.rem(tier + k, ntier)

    def tile_at(k):
        return lax.rem(tile + k, ntile)

    def window(index):
        return pl.ds(pl.multiple_of(index * cols, TILE_COLS), cols)

    def group(index):
        return pl.ds(pl.multiple_of(index * lev, 8), lev)

    barrier = pltpu.get_barrier_semaphore()
    for k in range(1, ntier):
        pl.semaphore_signal(barrier, inc=1, device_id={"tier": tier_at(k)}, device_id_type=MESH)

    def greet(k, carry):
        pl.semaphore_signal(barrier, inc=1, device_id={"tile": tile_at(k)}, device_id_type=MESH)
        return carry

    lax.fori_loop(1, ntile, greet, 0)

    def lookup(codes, axes):
        outs = [jnp.full(codes.shape, rates[a, 0], jnp.float32) for a in axes]
        for m in range(1, nmat):
            hit = codes == m
            outs = [jnp.where(hit, rates[a, m], o) for a, o in zip(axes, outs)]
        return outs

    lane = lax.broadcasted_iota(jnp.int32, (lev, TILE_COLS), 1)
    pair = lane >> 1

    def pack_edges(src, dst):
        for d in range(ntier):
            low = max(d * cols - TILE_COLS, 0)
            high = min((d + 1) * cols, width - TILE_COLS)
            acc = jnp.zeros((lev, TILE_COLS), src.dtype)
            for r in range(rows):
                both = jnp.where(
                    lane == TILE_COLS - 1,
                    src[r, :, low : low + TILE_COLS],
                    src[r, :, high : high + TILE_COLS],
                )
                acc = jnp.where(pair == r, pltpu.roll(both, 2 * r + 1, 1), acc)
            dst[d] = acc

    blk1 = lax.broadcasted_iota(jnp.int32, (1, nblk), 1)
    blkn = lax.broadcasted_iota(jnp.int32, (ntier, nblk), 1)

    sums = jnp.zeros((1, nblk), jnp.float32)
    areas = jnp.zeros((1, nblk), jnp.float32)
    active = t_in[0, 0:1, :]
    for r in range(1, rows):
        active = active + t_in[r, 0:1, :]
    for j in range(width // TILE_COLS):
        part = jnp.sum(active[:, j * TILE_COLS : (j + 1) * TILE_COLS], axis=1, keepdims=True)
        hit = blk1 == labels[0, j]
        sums = sums + jnp.where(hit, part, 0.0)
        areas = areas + jnp.where(hit, float(rows * TILE_COLS), 0.0)
    p1[0] = jnp.zeros(p1.shape[1:], jnp.float32)
    p1[0, 0:1, 0:nblk] = sums
    p1[0, 1:2, 0:nblk] = areas
    pack_edges(m_in, e_mat)

    pl.semaphore_wait(barrier, ntier - 1 + ntile - 1)

    def share(buf, s_sem, r_sem):
        def send(k, carry):
            pltpu.make_async_remote_copy(
                src_ref=buf.at[0], dst_ref=buf.at[k], send_sem=s_sem, recv_sem=r_sem,
                device_id={"tile": tile_at(k)}, device_id_type=MESH,
            ).start()
            return carry

        lax.fori_loop(1, ntile, send, 0)

    def shared(buf, r_sem):
        rest = buf.at[pl.ds(1, ntile - 1)]
        pltpu.make_async_copy(rest, rest, r_sem).wait()

    def total(buf):
        return lax.fori_loop(1, ntile, lambda k, acc: acc + buf[k], buf[0])

    share(p1, s_p1, r_p1)

    def halo_copies(low_src, high_src, dst, which):
        down = pltpu.make_async_remote_copy(
            src_ref=low_src, dst_ref=dst.at[1],
            send_sem=s_halo.at[which, 0], recv_sem=r_halo.at[which, 1],
            device_id={"tile": lax.max(tile - 1, 0)}, device_id_type=MESH,
        )
        up = pltpu.make_async_remote_copy(
            src_ref=high_src, dst_ref=dst.at[0],
            send_sem=s_halo.at[which, 1], recv_sem=r_halo.at[which, 0],
            device_id={"tile": lax.min(tile + 1, ntile - 1)}, device_id_type=MESH,
        )
        return down, up

    has_low = tile > 0
    has_high = tile < ntile - 1

    def halo_start(copies):
        pl.when(has_low)(lambda: copies[0].start())
        pl.when(has_high)(lambda: copies[1].start())

    def halo_recv(copies):
        pl.when(has_low)(lambda: copies[1].wait_recv())
        pl.when(has_high)(lambda: copies[0].wait_recv())

    def halo_sent(copies):
        pl.when(has_low)(lambda: copies[0].wait_send())
        pl.when(has_high)(lambda: copies[1].wait_send())

    @pl.when(jnp.logical_not(has_low))
    def _():
        halo_t[0] = jnp.zeros(halo_t.shape[1:], jnp.float32)
        halo_m[0] = jnp.zeros(halo_m.shape[1:], jnp.int32)
        halo_1[0] = jnp.zeros(halo_1.shape[1:], jnp.float32)
        col_mh[0] = jnp.zeros(col_mh.shape[1:], jnp.int32)

    @pl.when(jnp.logical_not(has_high))
    def _():
        halo_t[1] = jnp.zeros(halo_t.shape[1:], jnp.float32)
        halo_m[1] = jnp.zeros(halo_m.shape[1:], jnp.int32)
        halo_1[1] = jnp.zeros(halo_1.shape[1:], jnp.float32)
        col_mh[1] = jnp.zeros(col_mh.shape[1:], jnp.int32)

    temp_halo = halo_copies(t_in.at[0], t_in.at[rows - 1], halo_t, 0)
    mat_halo = halo_copies(m_in.at[0], m_in.at[rows - 1], halo_m, 1)
    halo_start(temp_halo)
    halo_start(mat_halo)

    def to_tier(src, dst, s_sem, r_sem, k):
        return pltpu.make_async_remote_copy(
            src_ref=src, dst_ref=dst, send_sem=s_sem, recv_sem=r_sem,
            device_id={"tier": tier_at(k)}, device_id_type=MESH,
        )

    def mat_copy(k, receive):
        src = tier_at(ntier - k) if receive else tier
        return to_tier(
            m_in.at[:, :, window(tier_at(k))], col_m.at[:, group(src), :],
            s_mat.at[k], r_mat.at[k], k,
        )

    def edge_copy(k, receive, src_ref, dst_ref, s_sem, r_sem):
        src = tier_at(ntier - k) if receive else tier
        return to_tier(
            src_ref.at[tier_at(k)], dst_ref.at[group(src), :], s_sem.at[k], r_sem.at[k], k
        )

    def row_copy(r, k, receive):
        src = tier_at(ntier - k) if receive else tier
        return to_tier(
            mv.at[r, :, window(tier_at(k))], col.at[r, group(src), :],
            s_a2a.at[r, k], r_a2a.at[r, k], k,
        )

    def out_copy(r, k, receive):
        src = tier_at(ntier - k) if receive else tier
        return to_tier(
            res.at[r, group(tier_at(k)), :], out.at[r, :, window(src)],
            s_out.at[r, k], r_out.at[r, k], k,
        )

    for k in range(1, ntier):
        mat_copy(k, False).start()
        edge_copy(k, False, e_mat, col_me, s_me, r_me).start()
    col_m[:, group(tier), :] = m_in[:, :, window(tier)]
    col_me[group(tier), :] = e_mat[tier]

    wide = lax.broadcasted_iota(jnp.int32, (lev, width), 1)
    before = None
    for r in range(rows):
        kx, ky = lookup(m_in[r], (0, 1))
        here = t_in[r]
        flux = jnp.where(
            wide == width - 1, 0.0, face(ky, pltpu.roll(ky, width - 1, 1))
        ) * (pltpu.roll(here, width - 1, 1) - here)
        mv[r] = here + (flux - pltpu.roll(flux, 1, 1))
        if r > 0:
            flow = face(before, kx) * (here - t_in[r - 1])
            mv[r] -= flow
            mv[r - 1] += flow
        before = kx

    shared(p1, r_p1)
    whole = total(p1)
    count = whole[1:2, 0:nblk]
    power = stat[pl.ds(tier, 1), :] * jnp.exp(
        fac[pl.ds(tier, 1), :] * whole[0:1, 0:nblk] / count
    )
    gain = []
    for j in range(width // TILE_COLS):
        mine = jnp.sum(jnp.where(blk1 == labels[0, j], power, 0.0), axis=1, keepdims=True)
        gain.append(jnp.broadcast_to(SOURCE_GAIN * mine, (1, TILE_COLS)))
    gain = jnp.concatenate(gain, axis=1)
    for r in range(rows):
        mv[r, 0:1, :] += gain

    for r in order[:-2]:
        for k in range(1, ntier):
            row_copy(r, k, False).start()
        col[r, group(tier), :] = mv[r, :, window(tier)]

    halo_recv(temp_halo)
    halo_recv(mat_halo)
    for r, side, inside in ((0, 0, has_low), (rows - 1, 1, has_high)):
        (own,) = lookup(m_in[r], (0,))
        (other,) = lookup(halo_m[side], (0,))
        other = jnp.where(inside, other, 0.0)
        mv[r] += face(own, other) * (halo_t[side] - t_in[r])
        for k in range(1, ntier):
            row_copy(r, k, False).start()
        col[r, group(tier), :] = mv[r, :, window(tier)]
    pack_edges(mv, e_mv)
    for k in range(1, ntier):
        edge_copy(k, False, e_mv, col_e, s_e, r_e).start()
    col_e[group(tier), :] = e_mv[tier]

    for k in range(1, ntier):
        mat_copy(k, True).wait_recv()
        edge_copy(k, True, e_mat, col_me, s_me, r_me).wait_recv()
    col_halo = halo_copies(col_m.at[0], col_m.at[rows - 1], col_mh, 2)
    halo_start(col_halo)
    narrow = lax.broadcasted_iota(jnp.int32, (levels, cols), 1)
    (ke,) = lookup(col_me[...], (1,))
    ke_low = jnp.where(tier > 0, ke, 0.0)
    ke_high = jnp.where(tier < ntier - 1, ke, 0.0)

    def at_first(edges, r):
        return pltpu.roll(edges, (TILE_COLS - 2 * r) % TILE_COLS, 1)

    def at_last(edges, r):
        return pltpu.roll(edges, TILE_COLS - 2 - 2 * r, 1)

    def widen(block):
        return jnp.concatenate([block] * quarter, axis=1)

    for r in range(rows):
        kx, ky = lookup(col_m[r], (0, 1))
        beside = jnp.where(
            narrow == cols - 1, widen(at_last(ke_high, r)), pltpu.roll(ky, cols - 1, 1)
        )
        cy[r] = face(ky, beside)
        cl[r] = face(ky[:, :TILE_COLS], at_first(ke_low, r))
        if r > 0:
            cx[r] = face(before, kx)
        before = kx
    halo_recv(col_halo)
    for r, side, inside in ((0, 0, has_low), (rows - 1, 1, has_high)):
        (own,) = lookup(col_m[r], (0,))
        (other,) = lookup(col_mh[side], (0,))
        cx[r + side] = face(own, jnp.where(inside, other, 0.0))

    op = a_in[...]
    for r in order:
        for k in range(1, ntier):
            row_copy(r, k, True).wait_recv()
        t1[r] = solve(op, col[r])
    one_halo = halo_copies(t1.at[0], t1.at[rows - 1], halo_1, 3)
    halo_start(one_halo)

    sums = jnp.zeros((ntier, nblk), jnp.float32)
    lines = []
    for t in range(ntier):
        line = t1[0, t * lev : t * lev + 1, :]
        for r in range(1, rows):
            line = line + t1[r, t * lev : t * lev + 1, :]
        lines.append(line)
    lines = jnp.concatenate(lines, axis=0)
    for q in range(quarter):
        part = jnp.sum(lines[:, q * TILE_COLS : (q + 1) * TILE_COLS], axis=1, keepdims=True)
        sums = sums + jnp.where(blkn == labels[0, tier * quarter + q], part, 0.0)
    p2a[0] = jnp.zeros(p2a.shape[1:], jnp.float32)
    p2a[0, 0:ntier, 0:nblk] = sums

    def tier_sum(k):
        return to_tier(p2a.at[0], p2a.at[k], s_pa.at[k], r_pa.at[k], k)

    for k in range(1, ntier):
        tier_sum(k).start()

    for k in range(1, ntier):
        edge_copy(k, True, e_mv, col_e, s_e, r_e).wait_recv()
    edges = solve(op, col_e[...])

    for k in range(1, ntier):
        tier_sum(k).wait_recv()
    acc = p2a[0]
    for k in range(1, ntier):
        acc = acc + p2a[k]
    p2b[0] = acc
    share(p2b, s_pb, r_pb)

    for r in range(rows):
        here = t1[r]
        beside = jnp.where(
            narrow == cols - 1, widen(at_last(edges, r)), pltpu.roll(here, cols - 1, 1)
        )
        flux = cy[r] * (beside - here)
        first = cl[r] * (here[:, :TILE_COLS] - at_first(edges, r))
        mv2[r] = here + (flux - jnp.where(narrow == 0, widen(first), pltpu.roll(flux, 1, 1)))
        if r > 0:
            flow = cx[r] * (here - t1[r - 1])
            mv2[r] -= flow
            mv2[r - 1] += flow

    shared(p2b, r_pb)
    whole = total(p2b)
    power = stat[...] * jnp.exp(fac[...] * whole[0:ntier, 0:nblk] / count)
    mine = lax.broadcasted_iota(jnp.int32, (ntier, nblk), 0) == tier
    pw_out[...] = jnp.sum(jnp.where(mine, power, 0.0), axis=0, keepdims=True)
    gain = []
    for q in range(quarter):
        hit = blkn == labels[0, tier * quarter + q]
        g = jnp.sum(jnp.where(hit, power, 0.0), axis=1, keepdims=True)
        gain.append(jnp.broadcast_to(SOURCE_GAIN * g, (ntier, TILE_COLS)))
    gain = jnp.concatenate(gain, axis=1)
    for r in range(rows):
        for t in range(ntier):
            mv2[r, t * lev : t * lev + 1, :] += gain[t : t + 1, :]

    def finish(r):
        res[r] = solve(op, mv2[r])
        for k in range(1, ntier):
            out_copy(r, k, False).start()
        out[r, :, window(tier)] = res[r, group(tier), :]

    for r in order[:-2]:
        finish(r)
    halo_recv(one_halo)
    for r, side in ((0, 0), (rows - 1, 1)):
        mv2[r] += cx[r + side] * (halo_1[side] - t1[r])
        finish(r)

    for r in order:
        for k in range(1, ntier):
            out_copy(r, k, True).wait_recv()

    for copies in (temp_halo, mat_halo, col_halo, one_halo):
        halo_sent(copies)
    for k in range(1, ntier):
        mat_copy(k, False).wait_send()
        edge_copy(k, False, e_mat, col_me, s_me, r_me).wait_send()
        edge_copy(k, False, e_mv, col_e, s_e, r_e).wait_send()
        tier_sum(k).wait_send()
        for r in range(rows):
            row_copy(r, k, False).wait_send()
            out_copy(r, k, False).wait_send()
    shared(p1, s_p1)
    shared(p2b, s_pb)


def solution(mesh):
    ntier, ntile = mesh.shape["tier"], mesh.shape["tile"]

    def shards(temp, mats, rates, labels, stat, fac, op):
        rows, lev, width = temp.shape
        nblk = stat.shape[1]
        pad = -(-nblk // 128) * 128
        cols, levels = width // ntier, lev * ntier
        f32, i32 = jnp.float32, jnp.int32
        vm = lambda shape, dtype=f32: pltpu.VMEM(shape, dtype)
        dma = pltpu.SemaphoreType.DMA
        vmem = pl.BlockSpec(memory_space=pltpu.VMEM)
        smem = pl.BlockSpec(memory_space=pltpu.SMEM)
        return pl.pallas_call(
            functools.partial(kernel, ntier, ntile, nblk),
            out_shape=(
                jax.ShapeDtypeStruct(temp.shape, f32),
                jax.ShapeDtypeStruct((1, nblk), f32),
            ),
            in_specs=[vmem, vmem, smem, smem, vmem, vmem, vmem],
            out_specs=(vmem, vmem),
            scratch_shapes=[
                vm((2, lev, width)), vm((2, lev, width), i32), vm((rows, lev, width)),
                vm((ntier, lev, TILE_COLS), i32), vm((ntier, lev, TILE_COLS)),
                vm((rows, levels, cols), i32), vm((levels, TILE_COLS), i32),
                vm((2, levels, cols), i32),
                vm((rows, levels, cols)), vm((levels, TILE_COLS)), vm((rows, levels, cols)),
                vm((2, levels, cols)), vm((rows, levels, cols)), vm((rows, levels, cols)),
                vm((rows + 1, levels, cols)), vm((rows, levels, cols)),
                vm((rows, levels, TILE_COLS)),
                vm((ntile, 8, pad)), vm((ntier, 8, pad)), vm((ntile, 8, pad)),
                dma((4, 2)), dma((4, 2)), dma((rows, ntier)), dma((rows, ntier)),
                dma((ntier,)), dma((ntier,)), dma((ntier,)), dma((ntier,)),
                dma((ntier,)), dma((ntier,)), dma((rows, ntier)), dma((rows, ntier)),
                dma, dma, dma((ntier,)), dma((ntier,)), dma, dma,
            ],
            compiler_params=pltpu.CompilerParams(
                collective_id=0, has_side_effects=True, vmem_limit_bytes=40 * 1024 * 1024
            ),
        )(temp, mats, rates, labels, stat, fac, op)

    return jax.shard_map(
        shards,
        mesh=mesh,
        in_specs=(P("tile", "tier", None), P("tile", "tier", None), P(), P("tile", None), P(), P(), P()),
        out_specs=(P("tile", "tier", None), P("tier", None)),
        check_vma=False,
    )
```

```python
import functools

import jax
import jax.numpy as jnp
from jax import lax
from jax.experimental import pallas as pl
from jax.experimental.pallas import tpu as pltpu
from jax.sharding import PartitionSpec as P

TILE_COLS = 128
LATERAL_RATE = 0.12
SOURCE_GAIN = 0.02
MESH = pl.DeviceIdType.MESH


def face(a, b):
    return (2.0 * LATERAL_RATE) * a * b / (a + b)


def solve(op, x):
    return jnp.dot(op, x, precision=lax.Precision.HIGHEST, preferred_element_type=jnp.float32)


def kernel(
    ntier, ntile, nblk,
    t_hbm, m_hbm, rates_hbm, labels_hbm, stat_hbm, fac_hbm, a_hbm,
    out, pw_out,
    t_in, m_in, rates, labels, stat, fac, a_in, s_in,
    halo_t, halo_m, mv, e_mat, e_mv, col_m, col_me, col_mh, col, col_e, t1, halo_1, mv2, res,
    cx, cy, cl, p1, p2a, p2b,
    s_halo, r_halo, s_a2a, r_a2a, s_mat, r_mat, s_me, r_me, s_e, r_e, s_out, r_out,
    s_p1, r_p1, s_pa, r_pa, s_pb, r_pb,
):
    tier = lax.axis_index("tier")
    tile = lax.axis_index("tile")
    rows, lev, width = t_in.shape
    cols = width // ntier
    quarter = cols // TILE_COLS
    levels = lev * ntier
    nmat = rates.shape[1]
    order = [r for r in range(1, rows - 1)] + [0, rows - 1]

    loads = [
        pltpu.make_async_copy(src, dst, s_in.at[i])
        for i, (src, dst) in enumerate(
            ((t_hbm, t_in), (m_hbm, m_in), (labels_hbm, labels), (rates_hbm, rates),
             (stat_hbm, stat), (fac_hbm, fac), (a_hbm, a_in))
        )
    ]
    for load in loads:
        load.start()

    def tier_at(k):
        return lax.rem(tier + k, ntier)

    def tile_at(k):
        return lax.rem(tile + k, ntile)

    def window(index):
        return pl.ds(pl.multiple_of(index * cols, TILE_COLS), cols)

    def group(index):
        return pl.ds(pl.multiple_of(index * lev, 8), lev)

    barrier = pltpu.get_barrier_semaphore()
    for k in range(1, ntier):
        pl.semaphore_signal(barrier, inc=1, device_id={"tier": tier_at(k)}, device_id_type=MESH)

    def greet(k, carry):
        pl.semaphore_signal(barrier, inc=1, device_id={"tile": tile_at(k)}, device_id_type=MESH)
        return carry

    lax.fori_loop(1, ntile, greet, 0)

    def lookup(codes, axes):
        outs = [jnp.full(codes.shape, rates[a, 0], jnp.float32) for a in axes]
        for m in range(1, nmat):
            hit = codes == m
            outs = [jnp.where(hit, rates[a, m], o) for a, o in zip(axes, outs)]
        return outs

    lane = lax.broadcasted_iota(jnp.int32, (lev, TILE_COLS), 1)
    pair = lane >> 1

    def pack_edges(src, dst):
        for d in range(ntier):
            low = max(d * cols - TILE_COLS, 0)
            high = min((d + 1) * cols, width - TILE_COLS)
            acc = jnp.zeros((lev, TILE_COLS), src.dtype)
            for r in range(rows):
                both = jnp.where(
                    lane == TILE_COLS - 1,
                    src[r, :, low : low + TILE_COLS],
                    src[r, :, high : high + TILE_COLS],
                )
                acc = jnp.where(pair == r, pltpu.roll(both, 2 * r + 1, 1), acc)
            dst[d] = acc

    blk1 = lax.broadcasted_iota(jnp.int32, (1, nblk), 1)
    blkn = lax.broadcasted_iota(jnp.int32, (ntier, nblk), 1)

    for load in loads:
        load.wait()
    sums = jnp.zeros((1, nblk), jnp.float32)
    areas = jnp.zeros((1, nblk), jnp.float32)
    active = t_in[0, 0:1, :]
    for r in range(1, rows):
        active = active + t_in[r, 0:1, :]
    for j in range(width // TILE_COLS):
        part = jnp.sum(active[:, j * TILE_COLS : (j + 1) * TILE_COLS], axis=1, keepdims=True)
        hit = blk1 == labels[0, j]
        sums = sums + jnp.where(hit, part, 0.0)
        areas = areas + jnp.where(hit, float(rows * TILE_COLS), 0.0)
    p1[0] = jnp.zeros(p1.shape[1:], jnp.float32)
    p1[0, 0:1, 0:nblk] = sums
    p1[0, 1:2, 0:nblk] = areas

    pl.semaphore_wait(barrier, ntier - 1 + ntile - 1)

    def share(buf, s_sem, r_sem):
        def send(k, carry):
            pltpu.make_async_remote_copy(
                src_ref=buf.at[0], dst_ref=buf.at[k], send_sem=s_sem, recv_sem=r_sem,
                device_id={"tile": tile_at(k)}, device_id_type=MESH,
            ).start()
            return carry

        lax.fori_loop(1, ntile, send, 0)

    def shared(buf, r_sem):
        rest = buf.at[pl.ds(1, ntile - 1)]
        pltpu.make_async_copy(rest, rest, r_sem).wait()

    def total(buf):
        return lax.fori_loop(1, ntile, lambda k, acc: acc + buf[k], buf[0])

    share(p1, s_p1, r_p1)

    def halo_copies(low_src, high_src, dst, which):
        down = pltpu.make_async_remote_copy(
            src_ref=low_src, dst_ref=dst.at[1],
            send_sem=s_halo.at[which, 0], recv_sem=r_halo.at[which, 1],
            device_id={"tile": lax.max(tile - 1, 0)}, device_id_type=MESH,
        )
        up = pltpu.make_async_remote_copy(
            src_ref=high_src, dst_ref=dst.at[0],
            send_sem=s_halo.at[which, 1], recv_sem=r_halo.at[which, 0],
            device_id={"tile": lax.min(tile + 1, ntile - 1)}, device_id_type=MESH,
        )
        return down, up

    has_low = tile > 0
    has_high = tile < ntile - 1

    def halo_start(copies):
        pl.when(has_low)(lambda: copies[0].start())
        pl.when(has_high)(lambda: copies[1].start())

    def halo_recv(copies):
        pl.when(has_low)(lambda: copies[1].wait_recv())
        pl.when(has_high)(lambda: copies[0].wait_recv())

    def halo_sent(copies):
        pl.when(has_low)(lambda: copies[0].wait_send())
        pl.when(has_high)(lambda: copies[1].wait_send())

    @pl.when(jnp.logical_not(has_low))
    def _():
        halo_t[0] = jnp.zeros(halo_t.shape[1:], jnp.float32)
        halo_m[0] = jnp.zeros(halo_m.shape[1:], jnp.int32)
        halo_1[0] = jnp.zeros(halo_1.shape[1:], jnp.float32)
        col_mh[0] = jnp.zeros(col_mh.shape[1:], jnp.int32)

    @pl.when(jnp.logical_not(has_high))
    def _():
        halo_t[1] = jnp.zeros(halo_t.shape[1:], jnp.float32)
        halo_m[1] = jnp.zeros(halo_m.shape[1:], jnp.int32)
        halo_1[1] = jnp.zeros(halo_1.shape[1:], jnp.float32)
        col_mh[1] = jnp.zeros(col_mh.shape[1:], jnp.int32)

    temp_halo = halo_copies(t_hbm.at[0], t_hbm.at[rows - 1], halo_t, 0)
    mat_halo = halo_copies(m_hbm.at[0], m_hbm.at[rows - 1], halo_m, 1)
    halo_start(temp_halo)
    halo_start(mat_halo)

    def to_tier(src, dst, s_sem, r_sem, k):
        return pltpu.make_async_remote_copy(
            src_ref=src, dst_ref=dst, send_sem=s_sem, recv_sem=r_sem,
            device_id={"tier": tier_at(k)}, device_id_type=MESH,
        )

    def mat_copy(k, receive):
        src = tier_at(ntier - k) if receive else tier
        return to_tier(
            m_hbm.at[:, :, window(tier_at(k))], col_m.at[:, group(src), :],
            s_mat.at[k], r_mat.at[k], k,
        )

    def edge_copy(k, receive, src_ref, dst_ref, s_sem, r_sem):
        src = tier_at(ntier - k) if receive else tier
        return to_tier(
            src_ref.at[tier_at(k)], dst_ref.at[group(src), :], s_sem.at[k], r_sem.at[k], k
        )

    def row_copy(r, k, receive):
        src = tier_at(ntier - k) if receive else tier
        return to_tier(
            mv.at[r, :, window(tier_at(k))], col.at[r, group(src), :],
            s_a2a.at[r, k], r_a2a.at[r, k], k,
        )

    def out_copy(r, k, receive):
        src = tier_at(ntier - k) if receive else tier
        return to_tier(
            res.at[r, group(tier_at(k)), :], out.at[r, :, window(src)],
            s_out.at[r, k], r_out.at[r, k], k,
        )

    for k in range(1, ntier):
        mat_copy(k, False).start()
    pack_edges(m_in, e_mat)
    for k in range(1, ntier):
        edge_copy(k, False, e_mat, col_me, s_me, r_me).start()
    col_m[:, group(tier), :] = m_in[:, :, window(tier)]
    col_me[group(tier), :] = e_mat[tier]

    wide = lax.broadcasted_iota(jnp.int32, (lev, width), 1)
    before = None
    for r in range(rows):
        kx, ky = lookup(m_in[r], (0, 1))
        here = t_in[r]
        flux = jnp.where(
            wide == width - 1, 0.0, face(ky, pltpu.roll(ky, width - 1, 1))
        ) * (pltpu.roll(here, width - 1, 1) - here)
        mv[r] = here + (flux - pltpu.roll(flux, 1, 1))
        if r > 0:
            flow = face(before, kx) * (here - t_in[r - 1])
            mv[r] -= flow
            mv[r - 1] += flow
        before = kx

    shared(p1, r_p1)
    whole = total(p1)
    count = whole[1:2, 0:nblk]
    power = stat[pl.ds(tier, 1), :] * jnp.exp(
        fac[pl.ds(tier, 1), :] * whole[0:1, 0:nblk] / count
    )
    gain = []
    for j in range(width // TILE_COLS):
        mine = jnp.sum(jnp.where(blk1 == labels[0, j], power, 0.0), axis=1, keepdims=True)
        gain.append(jnp.broadcast_to(SOURCE_GAIN * mine, (1, TILE_COLS)))
    gain = jnp.concatenate(gain, axis=1)
    for r in range(rows):
        mv[r, 0:1, :] += gain

    for r in order[:-2]:
        for k in range(1, ntier):
            row_copy(r, k, False).start()
        col[r, group(tier), :] = mv[r, :, window(tier)]

    halo_recv(temp_halo)
    halo_recv(mat_halo)
    for r, side, inside in ((0, 0, has_low), (rows - 1, 1, has_high)):
        (own,) = lookup(m_in[r], (0,))
        (other,) = lookup(halo_m[side], (0,))
        other = jnp.where(inside, other, 0.0)
        mv[r] += face(own, other) * (halo_t[side] - t_in[r])
        for k in range(1, ntier):
            row_copy(r, k, False).start()
        col[r, group(tier), :] = mv[r, :, window(tier)]
    pack_edges(mv, e_mv)
    for k in range(1, ntier):
        edge_copy(k, False, e_mv, col_e, s_e, r_e).start()
    col_e[group(tier), :] = e_mv[tier]

    for k in range(1, ntier):
        mat_copy(k, True).wait_recv()
        edge_copy(k, True, e_mat, col_me, s_me, r_me).wait_recv()
    col_halo = halo_copies(col_m.at[0], col_m.at[rows - 1], col_mh, 2)
    halo_start(col_halo)
    narrow = lax.broadcasted_iota(jnp.int32, (levels, cols), 1)
    (ke,) = lookup(col_me[...], (1,))
    ke_low = jnp.where(tier > 0, ke, 0.0)
    ke_high = jnp.where(tier < ntier - 1, ke, 0.0)

    def at_first(edges, r):
        return pltpu.roll(edges, (TILE_COLS - 2 * r) % TILE_COLS, 1)

    def at_last(edges, r):
        return pltpu.roll(edges, TILE_COLS - 2 - 2 * r, 1)

    def widen(block):
        return jnp.concatenate([block] * quarter, axis=1)

    for r in range(rows):
        kx, ky = lookup(col_m[r], (0, 1))
        beside = jnp.where(
            narrow == cols - 1, widen(at_last(ke_high, r)), pltpu.roll(ky, cols - 1, 1)
        )
        cy[r] = face(ky, beside)
        cl[r] = face(ky[:, :TILE_COLS], at_first(ke_low, r))
        if r > 0:
            cx[r] = face(before, kx)
        before = kx
    halo_recv(col_halo)
    for r, side, inside in ((0, 0, has_low), (rows - 1, 1, has_high)):
        (own,) = lookup(col_m[r], (0,))
        (other,) = lookup(col_mh[side], (0,))
        cx[r + side] = face(own, jnp.where(inside, other, 0.0))

    op = a_in[...]
    for r in order:
        for k in range(1, ntier):
            row_copy(r, k, True).wait_recv()
        t1[r] = solve(op, col[r])
    one_halo = halo_copies(t1.at[0], t1.at[rows - 1], halo_1, 3)
    halo_start(one_halo)

    sums = jnp.zeros((ntier, nblk), jnp.float32)
    lines = []
    for t in range(ntier):
        line = t1[0, t * lev : t * lev + 1, :]
        for r in range(1, rows):
            line = line + t1[r, t * lev : t * lev + 1, :]
        lines.append(line)
    lines = jnp.concatenate(lines, axis=0)
    for q in range(quarter):
        part = jnp.sum(lines[:, q * TILE_COLS : (q + 1) * TILE_COLS], axis=1, keepdims=True)
        sums = sums + jnp.where(blkn == labels[0, tier * quarter + q], part, 0.0)
    p2a[0] = jnp.zeros(p2a.shape[1:], jnp.float32)
    p2a[0, 0:ntier, 0:nblk] = sums

    def tier_sum(k):
        return to_tier(p2a.at[0], p2a.at[k], s_pa.at[k], r_pa.at[k], k)

    for k in range(1, ntier):
        tier_sum(k).start()

    for k in range(1, ntier):
        edge_copy(k, True, e_mv, col_e, s_e, r_e).wait_recv()
    edges = solve(op, col_e[...])

    for k in range(1, ntier):
        tier_sum(k).wait_recv()
    acc = p2a[0]
    for k in range(1, ntier):
        acc = acc + p2a[k]
    p2b[0] = acc
    share(p2b, s_pb, r_pb)

    for r in range(rows):
        here = t1[r]
        beside = jnp.where(
            narrow == cols - 1, widen(at_last(edges, r)), pltpu.roll(here, cols - 1, 1)
        )
        flux = cy[r] * (beside - here)
        first = cl[r] * (here[:, :TILE_COLS] - at_first(edges, r))
        mv2[r] = here + (flux - jnp.where(narrow == 0, widen(first), pltpu.roll(flux, 1, 1)))
        if r > 0:
            flow = cx[r] * (here - t1[r - 1])
            mv2[r] -= flow
            mv2[r - 1] += flow

    shared(p2b, r_pb)
    whole = total(p2b)
    power = stat[...] * jnp.exp(fac[...] * whole[0:ntier, 0:nblk] / count)
    mine = lax.broadcasted_iota(jnp.int32, (ntier, nblk), 0) == tier
    pw_out[...] = jnp.sum(jnp.where(mine, power, 0.0), axis=0, keepdims=True)
    gain = []
    for q in range(quarter):
        hit = blkn == labels[0, tier * quarter + q]
        g = jnp.sum(jnp.where(hit, power, 0.0), axis=1, keepdims=True)
        gain.append(jnp.broadcast_to(SOURCE_GAIN * g, (ntier, TILE_COLS)))
    gain = jnp.concatenate(gain, axis=1)
    for r in range(rows):
        for t in range(ntier):
            mv2[r, t * lev : t * lev + 1, :] += gain[t : t + 1, :]

    def finish(r):
        res[r] = solve(op, mv2[r])
        for k in range(1, ntier):
            out_copy(r, k, False).start()
        out[r, :, window(tier)] = res[r, group(tier), :]

    for r in order[:-2]:
        finish(r)
    halo_recv(one_halo)
    for r, side in ((0, 0), (rows - 1, 1)):
        mv2[r] += cx[r + side] * (halo_1[side] - t1[r])
        finish(r)

    for r in order:
        for k in range(1, ntier):
            out_copy(r, k, True).wait_recv()

    for copies in (temp_halo, mat_halo, col_halo, one_halo):
        halo_sent(copies)
    for k in range(1, ntier):
        mat_copy(k, False).wait_send()
        edge_copy(k, False, e_mat, col_me, s_me, r_me).wait_send()
        edge_copy(k, False, e_mv, col_e, s_e, r_e).wait_send()
        tier_sum(k).wait_send()
        for r in range(rows):
            row_copy(r, k, False).wait_send()
            out_copy(r, k, False).wait_send()
    shared(p1, s_p1)
    shared(p2b, s_pb)


def solution(mesh):
    ntier, ntile = mesh.shape["tier"], mesh.shape["tile"]

    def shards(temp, mats, rates, labels, stat, fac, op):
        rows, lev, width = temp.shape
        nblk = stat.shape[1]
        pad = -(-nblk // 128) * 128
        cols, levels = width // ntier, lev * ntier
        f32, i32 = jnp.float32, jnp.int32
        vm = lambda shape, dtype=f32: pltpu.VMEM(shape, dtype)
        dma = pltpu.SemaphoreType.DMA
        vmem = pl.BlockSpec(memory_space=pltpu.VMEM)
        return pl.pallas_call(
            functools.partial(kernel, ntier, ntile, nblk),
            out_shape=(
                jax.ShapeDtypeStruct(temp.shape, f32),
                jax.ShapeDtypeStruct((1, nblk), f32),
            ),
            in_specs=[pl.BlockSpec(memory_space=pltpu.HBM)] * 7,
            out_specs=(vmem, vmem),
            scratch_shapes=[
                vm(temp.shape), vm(mats.shape, i32), pltpu.SMEM(rates.shape, f32),
                pltpu.SMEM(labels.shape, i32), vm(stat.shape), vm(fac.shape), vm(op.shape),
                dma((7,)),
                vm((2, lev, width)), vm((2, lev, width), i32), vm((rows, lev, width)),
                vm((ntier, lev, TILE_COLS), i32), vm((ntier, lev, TILE_COLS)),
                vm((rows, levels, cols), i32), vm((levels, TILE_COLS), i32),
                vm((2, levels, cols), i32),
                vm((rows, levels, cols)), vm((levels, TILE_COLS)), vm((rows, levels, cols)),
                vm((2, levels, cols)), vm((rows, levels, cols)), vm((rows, levels, cols)),
                vm((rows + 1, levels, cols)), vm((rows, levels, cols)),
                vm((rows, levels, TILE_COLS)),
                vm((ntile, 8, pad)), vm((ntier, 8, pad)), vm((ntile, 8, pad)),
                dma((4, 2)), dma((4, 2)), dma((rows, ntier)), dma((rows, ntier)),
                dma((ntier,)), dma((ntier,)), dma((ntier,)), dma((ntier,)),
                dma((ntier,)), dma((ntier,)), dma((rows, ntier)), dma((rows, ntier)),
                dma, dma, dma((ntier,)), dma((ntier,)), dma, dma,
            ],
            compiler_params=pltpu.CompilerParams(
                collective_id=0, has_side_effects=True, vmem_limit_bytes=62 * 1024 * 1024
            ),
        )(temp, mats, rates, labels, stat, fac, op)

    return jax.shard_map(
        shards,
        mesh=mesh,
        in_specs=(P("tile", "tier", None), P("tile", "tier", None), P(), P("tile", None), P(), P(), P()),
        out_specs=(P("tile", "tier", None), P("tier", None)),
        check_vma=False,
    )
```

```python
import functools

import jax
import jax.numpy as jnp
from jax import lax
from jax.experimental import pallas as pl
from jax.experimental.pallas import tpu as pltpu
from jax.sharding import PartitionSpec as P

TILE_COLS = 128
LATERAL_RATE = 0.12
SOURCE_GAIN = 0.02
MESH = pl.DeviceIdType.MESH


def face(a, b):
    return (2.0 * LATERAL_RATE) * a * b / (a + b)


def solve(op, x):
    return jnp.dot(op, x, precision=lax.Precision.HIGHEST, preferred_element_type=jnp.float32)


def kernel(
    ntier, ntile, nblk,
    t_hbm, m_hbm, rates_hbm, labels_hbm, stat_hbm, fac_hbm, a_hbm,
    out, pw_out,
    t_in, m_in, rates, labels, stat, fac, a_in, s_in,
    halo_t, halo_m, mv, e_mat, e_mv, col_m, col_me, col_mh, col, col_e, t1, halo_1, mv2, res,
    cx, cy, cl, by_block, p1, p2a, p2b,
    s_halo, r_halo, s_a2a, r_a2a, s_mat, r_mat, s_me, r_me, s_e, r_e, s_out, r_out,
    s_p1, r_p1, s_pa, r_pa, s_pb, r_pb,
):
    tier = lax.axis_index("tier")
    tile = lax.axis_index("tile")
    rows, lev, width = t_in.shape
    cols = width // ntier
    quarter = cols // TILE_COLS
    levels = lev * ntier
    nmat = rates.shape[1]
    order = [r for r in range(1, rows - 1)] + [0, rows - 1]

    loads = [
        pltpu.make_async_copy(src, dst, s_in.at[i])
        for i, (src, dst) in enumerate(
            ((t_hbm, t_in), (m_hbm, m_in), (labels_hbm, labels), (rates_hbm, rates),
             (stat_hbm, stat), (fac_hbm, fac), (a_hbm, a_in))
        )
    ]
    for load in loads:
        load.start()

    def tier_at(k):
        return lax.rem(tier + k, ntier)

    def tile_at(k):
        return lax.rem(tile + k, ntile)

    def window(index):
        return pl.ds(pl.multiple_of(index * cols, TILE_COLS), cols)

    def group(index):
        return pl.ds(pl.multiple_of(index * lev, 8), lev)

    barrier = pltpu.get_barrier_semaphore()
    for k in range(1, ntier):
        pl.semaphore_signal(barrier, inc=1, device_id={"tier": tier_at(k)}, device_id_type=MESH)

    def greet(k, carry):
        pl.semaphore_signal(barrier, inc=1, device_id={"tile": tile_at(k)}, device_id_type=MESH)
        return carry

    lax.fori_loop(1, ntile, greet, 0)

    def lookup(codes, axes):
        outs = [jnp.full(codes.shape, rates[a, 0], jnp.float32) for a in axes]
        for m in range(1, nmat):
            hit = codes == m
            outs = [jnp.where(hit, rates[a, m], o) for a, o in zip(axes, outs)]
        return outs

    lane = lax.broadcasted_iota(jnp.int32, (lev, TILE_COLS), 1)
    pair = lane >> 1

    def pack_edges(src, dst):
        for d in range(ntier):
            low = max(d * cols - TILE_COLS, 0)
            high = min((d + 1) * cols, width - TILE_COLS)
            acc = jnp.zeros((lev, TILE_COLS), src.dtype)
            for r in range(rows):
                both = jnp.where(
                    lane == TILE_COLS - 1,
                    src[r, :, low : low + TILE_COLS],
                    src[r, :, high : high + TILE_COLS],
                )
                acc = jnp.where(pair == r, pltpu.roll(both, 2 * r + 1, 1), acc)
            dst[d] = acc

    blk1 = lax.broadcasted_iota(jnp.int32, (1, nblk), 1)
    blkn = lax.broadcasted_iota(jnp.int32, (ntier, nblk), 1)

    for load in loads:
        load.wait()
    sums = jnp.zeros((1, nblk), jnp.float32)
    areas = jnp.zeros((1, nblk), jnp.float32)
    active = t_in[0, 0:1, :]
    for r in range(1, rows):
        active = active + t_in[r, 0:1, :]
    for j in range(width // TILE_COLS):
        part = jnp.sum(active[:, j * TILE_COLS : (j + 1) * TILE_COLS], axis=1, keepdims=True)
        hit = blk1 == labels[0, j]
        sums = sums + jnp.where(hit, part, 0.0)
        areas = areas + jnp.where(hit, float(rows * TILE_COLS), 0.0)
    p1[0] = jnp.zeros(p1.shape[1:], jnp.float32)
    p1[0, 0:1, 0:nblk] = sums
    p1[0, 1:2, 0:nblk] = areas

    pl.semaphore_wait(barrier, ntier - 1 + ntile - 1)

    def share(buf, s_sem, r_sem):
        def send(k, carry):
            pltpu.make_async_remote_copy(
                src_ref=buf.at[0], dst_ref=buf.at[k], send_sem=s_sem, recv_sem=r_sem,
                device_id={"tile": tile_at(k)}, device_id_type=MESH,
            ).start()
            return carry

        lax.fori_loop(1, ntile, send, 0)

    def shared(buf, r_sem):
        rest = buf.at[pl.ds(1, ntile - 1)]
        pltpu.make_async_copy(rest, rest, r_sem).wait()

    def total(buf):
        return lax.fori_loop(1, ntile, lambda k, acc: acc + buf[k], buf[0])

    share(p1, s_p1, r_p1)

    def halo_copies(low_src, high_src, dst, which):
        down = pltpu.make_async_remote_copy(
            src_ref=low_src, dst_ref=dst.at[1],
            send_sem=s_halo.at[which, 0], recv_sem=r_halo.at[which, 1],
            device_id={"tile": lax.max(tile - 1, 0)}, device_id_type=MESH,
        )
        up = pltpu.make_async_remote_copy(
            src_ref=high_src, dst_ref=dst.at[0],
            send_sem=s_halo.at[which, 1], recv_sem=r_halo.at[which, 0],
            device_id={"tile": lax.min(tile + 1, ntile - 1)}, device_id_type=MESH,
        )
        return down, up

    has_low = tile > 0
    has_high = tile < ntile - 1

    def halo_start(copies):
        pl.when(has_low)(lambda: copies[0].start())
        pl.when(has_high)(lambda: copies[1].start())

    def halo_recv(copies):
        pl.when(has_low)(lambda: copies[1].wait_recv())
        pl.when(has_high)(lambda: copies[0].wait_recv())

    def halo_sent(copies):
        pl.when(has_low)(lambda: copies[0].wait_send())
        pl.when(has_high)(lambda: copies[1].wait_send())

    @pl.when(jnp.logical_not(has_low))
    def _():
        halo_t[0] = jnp.zeros(halo_t.shape[1:], jnp.float32)
        halo_m[0] = jnp.zeros(halo_m.shape[1:], jnp.int32)
        halo_1[0] = jnp.zeros(halo_1.shape[1:], jnp.float32)
        col_mh[0] = jnp.zeros(col_mh.shape[1:], jnp.int32)

    @pl.when(jnp.logical_not(has_high))
    def _():
        halo_t[1] = jnp.zeros(halo_t.shape[1:], jnp.float32)
        halo_m[1] = jnp.zeros(halo_m.shape[1:], jnp.int32)
        halo_1[1] = jnp.zeros(halo_1.shape[1:], jnp.float32)
        col_mh[1] = jnp.zeros(col_mh.shape[1:], jnp.int32)

    temp_halo = halo_copies(t_hbm.at[0], t_hbm.at[rows - 1], halo_t, 0)
    mat_halo = halo_copies(m_hbm.at[0], m_hbm.at[rows - 1], halo_m, 1)
    halo_start(temp_halo)
    halo_start(mat_halo)

    def to_tier(src, dst, s_sem, r_sem, k):
        return pltpu.make_async_remote_copy(
            src_ref=src, dst_ref=dst, send_sem=s_sem, recv_sem=r_sem,
            device_id={"tier": tier_at(k)}, device_id_type=MESH,
        )

    def mat_copy(k, receive):
        src = tier_at(ntier - k) if receive else tier
        return to_tier(
            m_hbm.at[:, :, window(tier_at(k))], col_m.at[:, group(src), :],
            s_mat.at[k], r_mat.at[k], k,
        )

    def edge_copy(k, receive, src_ref, dst_ref, s_sem, r_sem):
        src = tier_at(ntier - k) if receive else tier
        return to_tier(
            src_ref.at[tier_at(k)], dst_ref.at[group(src), :], s_sem.at[k], r_sem.at[k], k
        )

    def row_copy(r, k, receive):
        src = tier_at(ntier - k) if receive else tier
        return to_tier(
            mv.at[r, :, window(tier_at(k))], col.at[r, group(src), :],
            s_a2a.at[r, k], r_a2a.at[r, k], k,
        )

    def out_copy(r, k, receive):
        src = tier_at(ntier - k) if receive else tier
        return to_tier(
            res.at[r, group(tier_at(k)), :], out.at[r, :, window(src)],
            s_out.at[r, k], r_out.at[r, k], k,
        )

    for k in range(1, ntier):
        mat_copy(k, False).start()
    pack_edges(m_in, e_mat)
    for k in range(1, ntier):
        edge_copy(k, False, e_mat, col_me, s_me, r_me).start()
    col_m[:, group(tier), :] = m_in[:, :, window(tier)]
    col_me[group(tier), :] = e_mat[tier]

    wide = lax.broadcasted_iota(jnp.int32, (lev, width), 1)
    before = None
    for r in range(rows):
        kx, ky = lookup(m_in[r], (0, 1))
        here = t_in[r]
        flux = jnp.where(
            wide == width - 1, 0.0, face(ky, pltpu.roll(ky, width - 1, 1))
        ) * (pltpu.roll(here, width - 1, 1) - here)
        mv[r] = here + (flux - pltpu.roll(flux, 1, 1))
        if r > 0:
            flow = face(before, kx) * (here - t_in[r - 1])
            mv[r] -= flow
            mv[r - 1] += flow
        before = kx

    shared(p1, r_p1)
    whole = total(p1)
    count = whole[1:2, 0:nblk]
    power = stat[pl.ds(tier, 1), :] * jnp.exp(
        fac[pl.ds(tier, 1), :] * whole[0:1, 0:nblk] / count
    )
    gain = []
    for j in range(width // TILE_COLS):
        mine = jnp.sum(jnp.where(blk1 == labels[0, j], power, 0.0), axis=1, keepdims=True)
        gain.append(jnp.broadcast_to(SOURCE_GAIN * mine, (1, TILE_COLS)))
    gain = jnp.concatenate(gain, axis=1)
    for r in range(rows):
        mv[r, 0:1, :] += gain

    for r in order[:-2]:
        for k in range(1, ntier):
            row_copy(r, k, False).start()
        col[r, group(tier), :] = mv[r, :, window(tier)]

    halo_recv(temp_halo)
    halo_recv(mat_halo)
    for r, side, inside in ((0, 0, has_low), (rows - 1, 1, has_high)):
        (own,) = lookup(m_in[r], (0,))
        (other,) = lookup(halo_m[side], (0,))
        other = jnp.where(inside, other, 0.0)
        mv[r] += face(own, other) * (halo_t[side] - t_in[r])
        for k in range(1, ntier):
            row_copy(r, k, False).start()
        col[r, group(tier), :] = mv[r, :, window(tier)]
    pack_edges(mv, e_mv)
    for k in range(1, ntier):
        edge_copy(k, False, e_mv, col_e, s_e, r_e).start()
    col_e[group(tier), :] = e_mv[tier]

    level_sums = mv[0] + mv[1]
    for r in range(2, rows):
        level_sums = level_sums + mv[r]
    blkl = lax.broadcasted_iota(jnp.int32, (lev, nblk), 1)
    sums = jnp.zeros((lev, nblk), jnp.float32)
    for j in range(width // TILE_COLS):
        part = jnp.sum(
            level_sums[:, j * TILE_COLS : (j + 1) * TILE_COLS], axis=1, keepdims=True
        )
        sums = sums + jnp.where(blkl == labels[0, j], part, 0.0)
    by_block[...] = jnp.zeros_like(by_block)
    by_block[group(tier), :] = sums
    op = a_in[...]
    active_rows = jnp.concatenate(
        [op[t * lev : t * lev + 1, :] for t in range(ntier)]
        + [jnp.zeros((8 - ntier, levels), jnp.float32)],
        axis=0,
    )
    p2a[0] = jnp.zeros(p2a.shape[1:], jnp.float32)
    p2a[0, :, 0:nblk] = solve(active_rows, by_block[...])

    def tier_sum(k):
        return to_tier(p2a.at[0], p2a.at[k], s_pa.at[k], r_pa.at[k], k)

    for k in range(1, ntier):
        tier_sum(k).start()

    for k in range(1, ntier):
        mat_copy(k, True).wait_recv()
        edge_copy(k, True, e_mat, col_me, s_me, r_me).wait_recv()
    col_halo = halo_copies(col_m.at[0], col_m.at[rows - 1], col_mh, 2)
    halo_start(col_halo)
    narrow = lax.broadcasted_iota(jnp.int32, (levels, cols), 1)
    (ke,) = lookup(col_me[...], (1,))
    ke_low = jnp.where(tier > 0, ke, 0.0)
    ke_high = jnp.where(tier < ntier - 1, ke, 0.0)

    def at_first(edges, r):
        return pltpu.roll(edges, (TILE_COLS - 2 * r) % TILE_COLS, 1)

    def at_last(edges, r):
        return pltpu.roll(edges, TILE_COLS - 2 - 2 * r, 1)

    def widen(block):
        return jnp.concatenate([block] * quarter, axis=1)

    for r in range(rows):
        kx, ky = lookup(col_m[r], (0, 1))
        beside = jnp.where(
            narrow == cols - 1, widen(at_last(ke_high, r)), pltpu.roll(ky, cols - 1, 1)
        )
        cy[r] = face(ky, beside)
        cl[r] = face(ky[:, :TILE_COLS], at_first(ke_low, r))
        if r > 0:
            cx[r] = face(before, kx)
        before = kx
    for k in range(1, ntier):
        tier_sum(k).wait_recv()
    acc = p2a[0]
    for k in range(1, ntier):
        acc = acc + p2a[k]
    p2b[0] = acc
    share(p2b, s_pb, r_pb)

    for r in order:
        for k in range(1, ntier):
            row_copy(r, k, True).wait_recv()
        t1[r] = solve(op, col[r])
    one_halo = halo_copies(t1.at[0], t1.at[rows - 1], halo_1, 3)
    halo_start(one_halo)

    for k in range(1, ntier):
        edge_copy(k, True, e_mv, col_e, s_e, r_e).wait_recv()
    edges = solve(op, col_e[...])

    for r in range(rows):
        here = t1[r]
        beside = jnp.where(
            narrow == cols - 1, widen(at_last(edges, r)), pltpu.roll(here, cols - 1, 1)
        )
        flux = cy[r] * (beside - here)
        first = cl[r] * (here[:, :TILE_COLS] - at_first(edges, r))
        mv2[r] = here + (flux - jnp.where(narrow == 0, widen(first), pltpu.roll(flux, 1, 1)))
        if r > 0:
            flow = cx[r] * (here - t1[r - 1])
            mv2[r] -= flow
            mv2[r - 1] += flow

    shared(p2b, r_pb)
    whole = total(p2b)
    power = stat[...] * jnp.exp(fac[...] * whole[0:ntier, 0:nblk] / count)
    mine = lax.broadcasted_iota(jnp.int32, (ntier, nblk), 0) == tier
    pw_out[...] = jnp.sum(jnp.where(mine, power, 0.0), axis=0, keepdims=True)
    gain = []
    for q in range(quarter):
        hit = blkn == labels[0, tier * quarter + q]
        g = jnp.sum(jnp.where(hit, power, 0.0), axis=1, keepdims=True)
        gain.append(jnp.broadcast_to(SOURCE_GAIN * g, (ntier, TILE_COLS)))
    gain = jnp.concatenate(gain, axis=1)
    for r in range(rows):
        for t in range(ntier):
            mv2[r, t * lev : t * lev + 1, :] += gain[t : t + 1, :]

    def finish(r):
        res[r] = solve(op, mv2[r])
        for k in range(1, ntier):
            out_copy(r, k, False).start()
        out[r, :, window(tier)] = res[r, group(tier), :]

    for r in order[:-2]:
        finish(r)
    halo_recv(col_halo)
    for r, side, inside in ((0, 0, has_low), (rows - 1, 1, has_high)):
        (own,) = lookup(col_m[r], (0,))
        (other,) = lookup(col_mh[side], (0,))
        cx[r + side] = face(own, jnp.where(inside, other, 0.0))
    halo_recv(one_halo)
    for r, side in ((0, 0), (rows - 1, 1)):
        mv2[r] += cx[r + side] * (halo_1[side] - t1[r])
        finish(r)

    for r in order:
        for k in range(1, ntier):
            out_copy(r, k, True).wait_recv()

    for copies in (temp_halo, mat_halo, col_halo, one_halo):
        halo_sent(copies)
    for k in range(1, ntier):
        mat_copy(k, False).wait_send()
        edge_copy(k, False, e_mat, col_me, s_me, r_me).wait_send()
        edge_copy(k, False, e_mv, col_e, s_e, r_e).wait_send()
        tier_sum(k).wait_send()
        for r in range(rows):
            row_copy(r, k, False).wait_send()
            out_copy(r, k, False).wait_send()
    shared(p1, s_p1)
    shared(p2b, s_pb)


def solution(mesh):
    ntier, ntile = mesh.shape["tier"], mesh.shape["tile"]

    def shards(temp, mats, rates, labels, stat, fac, op):
        rows, lev, width = temp.shape
        nblk = stat.shape[1]
        pad = -(-nblk // 128) * 128
        cols, levels = width // ntier, lev * ntier
        f32, i32 = jnp.float32, jnp.int32
        vm = lambda shape, dtype=f32: pltpu.VMEM(shape, dtype)
        dma = pltpu.SemaphoreType.DMA
        vmem = pl.BlockSpec(memory_space=pltpu.VMEM)
        return pl.pallas_call(
            functools.partial(kernel, ntier, ntile, nblk),
            out_shape=(
                jax.ShapeDtypeStruct(temp.shape, f32),
                jax.ShapeDtypeStruct((1, nblk), f32),
            ),
            in_specs=[pl.BlockSpec(memory_space=pltpu.HBM)] * 7,
            out_specs=(vmem, vmem),
            scratch_shapes=[
                vm(temp.shape), vm(mats.shape, i32), pltpu.SMEM(rates.shape, f32),
                pltpu.SMEM(labels.shape, i32), vm(stat.shape), vm(fac.shape), vm(op.shape),
                dma((7,)),
                vm((2, lev, width)), vm((2, lev, width), i32), vm((rows, lev, width)),
                vm((ntier, lev, TILE_COLS), i32), vm((ntier, lev, TILE_COLS)),
                vm((rows, levels, cols), i32), vm((levels, TILE_COLS), i32),
                vm((2, levels, cols), i32),
                vm((rows, levels, cols)), vm((levels, TILE_COLS)), vm((rows, levels, cols)),
                vm((2, levels, cols)), vm((rows, levels, cols)), vm((rows, levels, cols)),
                vm((rows + 1, levels, cols)), vm((rows, levels, cols)),
                vm((rows, levels, TILE_COLS)),
                vm((levels, nblk)), vm((ntile, 8, pad)), vm((ntier, 8, pad)), vm((ntile, 8, pad)),
                dma((4, 2)), dma((4, 2)), dma((rows, ntier)), dma((rows, ntier)),
                dma((ntier,)), dma((ntier,)), dma((ntier,)), dma((ntier,)),
                dma((ntier,)), dma((ntier,)), dma((rows, ntier)), dma((rows, ntier)),
                dma, dma, dma((ntier,)), dma((ntier,)), dma, dma,
            ],
            compiler_params=pltpu.CompilerParams(
                collective_id=0, has_side_effects=True, vmem_limit_bytes=62 * 1024 * 1024
            ),
        )(temp, mats, rates, labels, stat, fac, op)

    return jax.shard_map(
        shards,
        mesh=mesh,
        in_specs=(P("tile", "tier", None), P("tile", "tier", None), P(), P("tile", None), P(), P(), P()),
        out_specs=(P("tile", "tier", None), P("tier", None)),
        check_vma=False,
    )
```
